1024 devices in a mesh: node: 128 (over z, x, core), local: 8 (over y).
Axes of the slice: x: 4, y: 8, z: 16, core: 2. Of those that a mesh axis runs over, the one named last changes fastest.
Arguments:
- grad_out: bfloat16 [4096, 3584], P('node', 'local'), may hold values from -6 to 6
- expert_ids: int32 [4096, 8], replicated, may hold values from 0 to 255, as said below
- row_slots: int32 [4096, 8], replicated, may hold values from 0 to 127, as said below
- combine: float32 [4096, 8], replicated, may hold values from 0.2 to 1.5
- down_weight: bfloat16 [256, 1024, 3584], P('node', None, 'local'), may hold values from -0.09375 to 0.09375
- gate_pre: bfloat16 [256, 128, 1024], P('node', None, 'local'), may hold values from -6 to 6
- up_pre: bfloat16 [256, 128, 1024], P('node', None, 'local'), may hold values from -3 to 3
Outputs:
- d_gate: bfloat16 [256, 128, 1024], P('node', None, 'local')
- d_up: bfloat16 [256, 128, 1024], P('node', None, 'local')
- d_combine: float32 [4096, 8], P('node')
The draws below stay inside these ranges and needn't reach their ends.
Inputs may be any that keep to these rules, and one draw needn't show every extreme that they name: `expert_ids`: each token names 8 different experts, two on each of 4 nodes (expert e lies on node e // 2). The tokens of one index of node choose any one node in at most 1 token, and some pair of nodes reaches 1. `row_slots`: every pair of an expert and a row is named by exactly one choice of one token.
All inputs are finite; a program needn't handle non-finite values.
Results may differ from the reference program's by a relative error of at most 0.0015.
Values may be sent and summed in bfloat16 or wider, within the bound.
A program may use at most 32 MiB of HBM per device.

```python
import math
import jax
import jax.numpy as jnp
from jax import lax

D = 3584
HID = 1024
TOPK = 8
EXP_NODE = 2
TOK_NODE = 32
EXPERTS = 256
TOKENS = 4096
CAP = 128
N_NODE = 128


def routing(key):
    per_token = TOPK // EXP_NODE
    quarter = N_NODE // per_token
    relabel = jax.random.permutation(jax.random.fold_in(key, 11), N_NODE).astype(jnp.int32)
    offset_all = jax.random.randint(jax.random.fold_in(key, 12), (), 0, N_NODE)
    local_keys = jax.random.randint(jax.random.fold_in(key, 13), (N_NODE, TOK_NODE), 0, 1000) * TOK_NODE + jnp.arange(TOK_NODE)[None, :]
    local_perm = jnp.argsort(local_keys, axis=1).astype(jnp.int32)
    virt_node = jnp.arange(N_NODE, dtype=jnp.int32)[:, None, None]
    virt_tok = jnp.arange(TOK_NODE, dtype=jnp.int32)[None, :, None]
    column = jnp.arange(per_token, dtype=jnp.int32)[None, None, :]
    dest_virt = (virt_node + virt_tok + column * quarter + offset_all) % N_NODE
    dest_node = relabel[dest_virt]
    row_index = virt_tok * per_token + column
    member = jnp.arange(EXP_NODE, dtype=jnp.int32)
    expert = (EXP_NODE * dest_node[..., None] + member).reshape(N_NODE, TOK_NODE, TOPK)
    row_full = jnp.broadcast_to(row_index[..., None], (N_NODE, TOK_NODE, per_token, EXP_NODE)).reshape(N_NODE, TOK_NODE, TOPK)
    slot_shift = jax.random.randint(jax.random.fold_in(key, 14), (EXPERTS,), 0, CAP)
    slot = (row_full + slot_shift[expert]) % CAP
    scores = jax.random.randint(jax.random.fold_in(key, 15), (N_NODE, TOK_NODE, TOPK), 0, 1000) * TOPK + jnp.arange(TOPK)[None, None, :]
    within = jnp.argsort(scores, axis=2)
    expert = jnp.take_along_axis(expert, within, axis=2)
    slot = jnp.take_along_axis(slot, within, axis=2)
    token_index = (relabel[:, None] * TOK_NODE + local_perm).reshape(-1)
    expert_out = jnp.zeros((TOKENS, TOPK), jnp.int32).at[token_index].set(expert.reshape(TOKENS, TOPK).astype(jnp.int32))
    slot_out = jnp.zeros((TOKENS, TOPK), jnp.int32).at[token_index].set(slot.reshape(TOKENS, TOPK).astype(jnp.int32))
    return (expert_out, slot_out)


def draw_expert_ids(key, part):
    expert, slot = routing(key)
    return expert


def draw_row_slots(key, part):
    expert, slot = routing(key)
    return slot


def block_levels(key, extent, cuts, least, high):
    def one(axis_at, shards_of):
        heights = jax.random.uniform(jax.random.fold_in(jax.random.fold_in(key, 6), axis_at), (shards_of,), jnp.float32, least / len(cuts), high / len(cuts))
        return jnp.repeat(jnp.exp(heights), extent[axis_at] // shards_of).reshape((-1,) + (1,) * (len(extent) - axis_at - 1))

    factor_of = one(*cuts[0])
    for cut in cuts[1:]:
        factor_of = factor_of * one(*cut)
    return factor_of


def scatter_about(key, dims, scale, bound, pieces=(), kind=jnp.bfloat16):
    array = scale * jax.random.normal(key, dims, jnp.float32)
    if pieces:
        array = array * block_levels(key, dims, pieces, -0.22, 0.18)
    return jnp.clip(array, -bound, bound).astype(kind)


def setup_inputs(seed: int = 0) -> dict:
    splits = jax.random.split(jax.random.key(seed), 8)
    grad_out = scatter_about(splits[0], (TOKENS, D), 1.0, 6.0, ((0, 128), (1, 8)))
    expert_ids = draw_expert_ids(jax.random.fold_in(splits[7], 71), 0)
    row_slots = draw_row_slots(jax.random.fold_in(splits[7], 71), 0)
    combine = jnp.clip(jnp.exp(jax.random.uniform(splits[3], (TOKENS, TOPK), jnp.float32, math.log(0.2), math.log(1.5))), 0.2, 1.5)
    down_weight = scatter_about(splits[4], (EXPERTS, HID, D), D ** -0.5, 0.09375, ((0, 128), (2, 8)))
    gate_pre = scatter_about(splits[5], (EXPERTS, CAP, HID), 1.0, 6.0, ((0, 128), (2, 8)))
    up_pre = scatter_about(splits[6], (EXPERTS, CAP, HID), 0.5, 3.0, ((0, 128), (2, 8)))
    return dict(grad_out=grad_out, expert_ids=expert_ids, row_slots=row_slots, combine=combine, down_weight=down_weight, gate_pre=gate_pre, up_pre=up_pre)


def expert_part(args):
    rows_e, weight_e, down_e, gate_e, up_e = args
    projected = jnp.dot(rows_e, down_e.T, preferred_element_type=jnp.float32)
    gate_wide = gate_e.astype(jnp.float32)
    up_wide = up_e.astype(jnp.float32)
    logistic = jax.nn.sigmoid(gate_wide)
    activated = gate_wide * logistic
    hidden = activated * up_wide
    grad_hidden = weight_e[:, None] * projected
    d_gate = (grad_hidden * up_wide * logistic * (1.0 + gate_wide * (1.0 - logistic))).astype(jnp.bfloat16)
    d_up = (grad_hidden * activated).astype(jnp.bfloat16)
    score = jnp.sum(hidden * projected, axis=1)
    return d_gate, d_up, score


def reference(grad_out, expert_ids, row_slots, combine, down_weight, gate_pre, up_pre):
    flat = (expert_ids * CAP + row_slots).astype(jnp.int32)
    owner = jnp.repeat(jnp.arange(TOKENS, dtype=jnp.int32), TOPK)
    row_token = jnp.zeros((EXPERTS * CAP,), jnp.int32).at[flat.reshape(-1)].set(owner)
    row_weight = jnp.zeros((EXPERTS * CAP,), jnp.float32).at[flat.reshape(-1)].set(combine.reshape(-1))
    rows = grad_out[row_token].reshape(EXPERTS, CAP, D)
    weight = row_weight.reshape(EXPERTS, CAP)
    d_gate, d_up, score = lax.map(expert_part, (rows, weight, down_weight, gate_pre, up_pre))
    d_combine = score.reshape(-1)[flat]
    return d_gate, d_up, d_combine
```

```python
import jax
import jax.numpy as jnp
from jax import lax
from jax.experimental import pallas as pl
from jax.experimental.pallas import tpu as pltpu
from jax.sharding import PartitionSpec as P

MESH = pl.DeviceIdType.MESH
NP = 8
NZ = 16
NN = NP * NZ
NL = 8
CAP = 128
HB = 128
DL = 448
DPAD = 512
F32 = jnp.float32
BF16 = jnp.bfloat16
EXACT = lax.Precision.HIGHEST


def dot(a, b):
    return jnp.dot(a, b, preferred_element_type=F32)


def one_hot(cond, dtype=BF16):
    return jnp.where(cond, 1.0, 0.0).astype(dtype)


def iota(shape, dim):
    return lax.broadcasted_iota(jnp.int32, shape, dim)


def turn(i):
    half = lax.div(i + 1, 2)
    return 4 + half * (1 - 2 * lax.rem(i, 2))


def kernel(
    ids_ref, slots_ref, comb_ref, g_ref, w_hbm, gate_ref, up_ref,
    dg_ref, du_ref, dc_ref,
    s1, r1, s2, r2, wv, xs, gm, gsel, a_gate, a_up, hid, qs, qr, cs, cr, acc,
    ys, yr, ps, pr, zs, zr,
    w_sem, s1_sem, r1_sem, s2_sem, r2_sem, qs_sem, qr_sem, cs_sem, cr_sem,
    ys_sem, yr_sem, ps_sem, pr_sem, zs_sem, zr_sem,
):
    node = lax.axis_index("node")
    loc = lax.axis_index("local")
    zi = lax.div(node, NP)
    pi = lax.rem(node, NP)

    w_copy = pltpu.make_async_copy(w_hbm, wv, w_sem)
    w_copy.start()

    def p_peer(d):
        return lax.rem(pi + d, NP)

    def z_peer(d):
        return lax.rem(zi + d, NZ)

    def l_peer(d):
        return lax.rem(loc + d, NL)

    barrier = pltpu.get_barrier_semaphore()

    def greet_p(d, c):
        pl.semaphore_signal(barrier, inc=1, device_id=(zi * NP + p_peer(d), loc), device_id_type=MESH)
        pl.semaphore_signal(barrier, inc=1, device_id=(node, l_peer(d)), device_id_type=MESH)
        return c

    def greet_z(d, c):
        pl.semaphore_signal(barrier, inc=1, device_id=(z_peer(d) * NP + pi, loc), device_id_type=MESH)
        return c

    lax.fori_loop(1, NP, greet_p, 0)
    lax.fori_loop(1, NZ, greet_z, 0)

    base = pl.multiple_of(lax.div(node, 4) * 128, 128)
    ids_c = ids_ref[:, pl.ds(base, 128)]
    sub = lax.rem(node, 4)
    ids_my = ids_c[:, 0:32]
    for j in range(1, 4):
        ids_my = jnp.where(sub == j, ids_c[:, 32 * j : 32 * j + 32], ids_my)
    dest = ids_my >> 1
    i = iota((NN, 32), 0)
    dest_of = (i & (NZ - 1)) * NP + (i >> 4)
    hit = jnp.zeros((NN, 32), F32)
    for k in range(8):
        hit = jnp.where(dest_of == dest[k : k + 1, :], 1.0, hit)
    x = dot(hit.astype(BF16), g_ref[...]).astype(BF16)
    s1[:, :, 0:DL] = x.reshape(NP, NZ, DL)
    s1[:, :, DL:DPAD] = jnp.zeros((NP, NZ, DPAD - DL), BF16)

    pl.semaphore_wait(barrier, 2 * (NP - 1) + NZ - 1)

    def s1_copy(d, src, dst):
        return pltpu.make_async_remote_copy(
            src_ref=s1.at[src], dst_ref=r1.at[dst],
            send_sem=s1_sem.at[d], recv_sem=r1_sem.at[d],
            device_id=(zi * NP + p_peer(d), loc), device_id_type=MESH,
        )

    def s1_start(d, c):
        s1_copy(d, p_peer(d), pi).start()
        return c

    lax.fori_loop(1, NP, s1_start, 0)
    r1[pl.ds(pi, 1)] = s1[pl.ds(pi, 1)]

    ri = iota((2 * NN, NN), 0)
    ci = iota((2 * NN, NN), 1)
    want = (ri & (NP - 1)) * NZ + (ri >> 4)
    half = (ri >> 3) & 1
    perm0 = one_hot((ci == want) & (half == 0))
    perm1 = one_hot((ci == want) & (half == 1))

    def s1_wait(d, c):
        s1_copy(d, p_peer(d), lax.rem(pi + NP - d, NP)).wait_recv()
        return c

    lax.fori_loop(1, NP, s1_wait, 0)
    r1f = r1[...].reshape(NN, DPAD)
    s2v = dot(perm0, r1f[:, 0:256]) + dot(perm1, r1f[:, 256:512])
    s2[...] = s2v.astype(BF16).reshape(NZ, 16, 256)

    def s2_copy(d, src, dst):
        return pltpu.make_async_remote_copy(
            src_ref=s2.at[src], dst_ref=r2.at[dst],
            send_sem=s2_sem.at[d], recv_sem=r2_sem.at[d],
            device_id=(z_peer(d) * NP + pi, loc), device_id_type=MESH,
        )

    def s2_start(d, c):
        s2_copy(d, z_peer(d), zi).start()
        return c

    lax.fori_loop(1, NZ, s2_start, 0)
    r2[pl.ds(zi, 1)] = s2[pl.ds(zi, 1)]

    ids = ids_ref[...]
    slots = slots_ref[...].astype(F32)
    comb = comb_ref[...]
    spread = (iota((128, NN), 0) >> 5) == (iota((128, NN), 1) & 3)
    spread_b = one_hot(spread)
    spread_f = one_hot(spread, F32)
    rows_here = (iota((256, NN), 0) >> 3) == (iota((256, NN), 1) >> 2)

    def stack(v):
        return jnp.concatenate([v[:, c * 128 : (c + 1) * 128] for c in range(32)], axis=0)

    nn = iota((NN, 256), 0)
    cc = iota((NN, 256), 1)
    place = (nn >> 3) * 16 + (nn & 7)
    ex0 = one_hot(cc == place)
    ex1 = one_hot(cc == place + 8)
    si = iota((CAP, NN), 0).astype(F32)
    for e in range(2):
        mine = ids == 2 * node + e
        slot_y = dot(stack(jnp.where(mine, slots, 0.0)).astype(BF16), spread_b)
        slot_n = jnp.sum(jnp.where(rows_here, slot_y, 0.0), axis=0, keepdims=True)
        comb_y = jnp.dot(
            stack(jnp.where(mine, comb, 0.0)), spread_f, precision=EXACT, preferred_element_type=F32
        )
        comb_n = jnp.sum(jnp.where(rows_here, comb_y, 0.0), axis=0, keepdims=True)
        sel = si == slot_n
        sel_f = jnp.where(sel, 1.0, 0.0)
        gm[e] = sel_f
        weight = jnp.sum(jnp.where(sel, comb_n, 0.0), axis=1, keepdims=True)
        sel_b = sel_f.astype(BF16)
        gsel[e, 0] = dot(sel_b, ex0).astype(BF16)
        gsel[e, 1] = dot(sel_b, ex1).astype(BF16)
        g = gate_ref[e].astype(F32)
        u = up_ref[e].astype(F32)
        sg = 1.0 / (1.0 + jnp.exp(-g))
        gs = g * sg
        hid[e] = gs * u
        a_up[e] = weight * gs
        a_gate[e] = weight * (u * sg * (1.0 + g * (1.0 - sg)))

    w_copy.wait()

    def s2_wait(d, c):
        s2_copy(d, z_peer(d), lax.rem(zi + NZ - d, NZ)).wait_recv()
        return c

    lax.fori_loop(1, NZ, s2_wait, 0)
    r2f = r2[...].reshape(256, 256)
    for e in range(2):
        xs[e, :, 0:256] = dot(gsel[e, 0], r2f).astype(BF16)
        xs[e, :, 256:512] = dot(gsel[e, 1], r2f).astype(BF16)

    def q_copy(d, src, dst):
        return pltpu.make_async_remote_copy(
            src_ref=qs.at[src], dst_ref=qr.at[dst],
            send_sem=qs_sem.at[d], recv_sem=qr_sem.at[d],
            device_id=(node, l_peer(d)), device_id_type=MESH,
        )

    def c_copy(d, src, dst):
        return pltpu.make_async_remote_copy(
            src_ref=cs.at[src], dst_ref=cr.at[dst],
            send_sem=cs_sem.at[d], recv_sem=cr_sem.at[d],
            device_id=(node, l_peer(d)), device_id_type=MESH,
        )

    def project(e, l):
        cols = pl.ds(pl.multiple_of(l * HB, HB), HB)
        return dot(xs[e, :, 0:DL], wv[e, :, cols])

    def send_block(i, c):
        d = turn(i)
        l = l_peer(d)
        for e in range(2):
            t = project(e, l)
            top = jnp.maximum(jnp.max(jnp.abs(t), axis=0, keepdims=True), 1e-30)
            q = jnp.round(t * (32767.0 / top))
            qs[l, e] = q.astype(jnp.int32).astype(jnp.int16)
            cs[l, e : e + 1, :] = top * (1.0 / 32767.0)
        c_copy(d, l, loc).start()
        q_copy(d, l, loc).start()
        return c

    lax.fori_loop(0, NL - 1, send_block, 0)
    for e in range(2):
        acc[e] = project(e, loc)

    def take_block(i, c):
        d = turn(i)
        l = lax.rem(loc + NL - d, NL)
        c_copy(d, l_peer(d), l).wait_recv()
        q_copy(d, l_peer(d), l).wait_recv()
        for e in range(2):
            acc[e] += qr[l, e].astype(jnp.int32).astype(F32) * cr[l, e : e + 1, :]
        return c

    lax.fori_loop(0, NL - 1, take_block, 0)

    for e in range(2):
        t = acc[e]
        part = jnp.sum(hid[e] * t, axis=1, keepdims=True)
        ys[e : e + 1, :] = jnp.sum(gm[e] * part, axis=0, keepdims=True)

    def y_copy(d, dst):
        return pltpu.make_async_remote_copy(
            src_ref=ys, dst_ref=yr.at[dst],
            send_sem=ys_sem.at[d], recv_sem=yr_sem.at[d],
            device_id=(node, l_peer(d)), device_id_type=MESH,
        )

    def y_start(d, c):
        y_copy(d, loc).start()
        return c

    lax.fori_loop(1, NL, y_start, 0)
    yr[pl.ds(loc, 1)] = ys[...].reshape(1, 2, NN)
    for e in range(2):
        t = acc[e]
        dg_ref[e] = (t * a_gate[e]).astype(BF16)
        du_ref[e] = (t * a_up[e]).astype(BF16)

    def y_wait(d, c):
        y_copy(d, lax.rem(loc + NL - d, NL)).wait_recv()
        return c

    lax.fori_loop(1, NL, y_wait, 0)
    ps[...] = jnp.sum(yr[...], axis=0)

    def p_copy(d, dst):
        return pltpu.make_async_remote_copy(
            src_ref=ps, dst_ref=pr.at[dst],
            send_sem=ps_sem.at[d], recv_sem=pr_sem.at[d],
            device_id=(zi * NP + p_peer(d), loc), device_id_type=MESH,
        )

    def p_start(d, c):
        p_copy(d, pi).start()
        return c

    lax.fori_loop(1, NP, p_start, 0)
    pr[pl.ds(pi, 1)] = ps[...].reshape(1, 2, NN)

    def p_wait(d, c):
        p_copy(d, lax.rem(pi + NP - d, NP)).wait_recv()
        return c

    lax.fori_loop(1, NP, p_wait, 0)
    to_here = (iota((2, NN), 1) & (NP - 1)) == pi
    packed = jnp.zeros((2, NN), F32)
    for q in range(NP):
        v = jnp.where(to_here, pr[q], 0.0)
        if q:
            v = jnp.concatenate([v[:, NN - q :], v[:, : NN - q]], axis=1)
        packed = packed + v
    zs[...] = packed

    def z_copy(d, dst):
        return pltpu.make_async_remote_copy(
            src_ref=zs, dst_ref=zr.at[dst],
            send_sem=zs_sem.at[d], recv_sem=zr_sem.at[d],
            device_id=(z_peer(d) * NP + pi, loc), device_id_type=MESH,
        )

    def z_start(d, c):
        z_copy(d, zi).start()
        return c

    lax.fori_loop(1, NZ, z_start, 0)
    zr[pl.ds(zi, 1)] = packed.reshape(1, 2, NN)

    choice = jnp.concatenate([ids_my[k : k + 1, :] for k in range(8)], axis=1)
    lane = (node + ((choice >> 1) & (NP - 1))) & (NN - 1)
    lane_hit = iota((NN, 256), 0) == lane
    plane_hit = iota((NZ, 256), 0) == (choice >> 4)
    member = choice & 1

    def z_wait(d, c):
        z_copy(d, lax.rem(zi + NZ - d, NZ)).wait_recv()
        return c

    lax.fori_loop(1, NZ, z_wait, 0)
    found = jnp.zeros((NN, 256), F32)
    for m in range(2):
        pick = jnp.where(plane_hit & (member == m), 1.0, 0.0)
        found = found + lax.dot_general(
            zr[:, m, :], pick, (((0,), (0,)), ((), ())), precision=EXACT, preferred_element_type=F32
        )
    flat = jnp.sum(jnp.where(lane_hit, found, 0.0), axis=0, keepdims=True)
    for k in range(8):
        dc_ref[k : k + 1, :] = flat[:, 32 * k : 32 * k + 32]

    def drain8(d, c):
        s1_copy(d, p_peer(d), pi).wait_send()
        q_copy(d, l_peer(d), loc).wait_send()
        c_copy(d, l_peer(d), loc).wait_send()
        y_copy(d, loc).wait_send()
        p_copy(d, pi).wait_send()
        return c

    def drain16(d, c):
        s2_copy(d, z_peer(d), zi).wait_send()
        z_copy(d, zi).wait_send()
        return c

    lax.fori_loop(1, NP, drain8, 0)
    lax.fori_loop(1, NZ, drain16, 0)


def shards(grad_out, expert_ids, row_slots, combine, down_weight, gate_pre, up_pre):
    vmem = pl.BlockSpec(memory_space=pltpu.VMEM)
    dma = pltpu.SemaphoreType.DMA
    d_gate, d_up, d_combine = pl.pallas_call(
        kernel,
        out_shape=(
            jax.ShapeDtypeStruct(gate_pre.shape, BF16),
            jax.ShapeDtypeStruct(gate_pre.shape, BF16),
            jax.ShapeDtypeStruct((8, 32), F32),
        ),
        in_specs=[vmem, vmem, vmem, vmem, pl.BlockSpec(memory_space=pl.ANY), vmem, vmem],
        out_specs=(vmem, vmem, vmem),
        scratch_shapes=[
            pltpu.VMEM((NP, NZ, DPAD), BF16),
            pltpu.VMEM((NP, NZ, DPAD), BF16),
            pltpu.VMEM((NZ, 16, 256), BF16),
            pltpu.VMEM((NZ, 16, 256), BF16),
            pltpu.VMEM((2, DL, 1024), BF16),
            pltpu.VMEM((2, CAP, DPAD), BF16),
            pltpu.VMEM((2, CAP, NN), F32),
            pltpu.VMEM((2, 2, CAP, 256), BF16),
            pltpu.VMEM((2, CAP, HB), F32),
            pltpu.VMEM((2, CAP, HB), F32),
            pltpu.VMEM((2, CAP, HB), F32),
            pltpu.VMEM((NL, 2, CAP, HB), jnp.int16),
            pltpu.VMEM((NL, 2, CAP, HB), jnp.int16),
            pltpu.VMEM((NL, 2, HB), F32),
            pltpu.VMEM((NL, 2, HB), F32),
            pltpu.VMEM((2, CAP, HB), F32),
            pltpu.VMEM((2, NN), F32),
            pltpu.VMEM((NL, 2, NN), F32),
            pltpu.VMEM((2, NN), F32),
            pltpu.VMEM((NP, 2, NN), F32),
            pltpu.VMEM((2, NN), F32),
            pltpu.VMEM((NZ, 2, NN), F32),
            dma,
            dma((NP,)), dma((NP,)),
            dma((NZ,)), dma((NZ,)),
            dma((NL,)), dma((NL,)),
            dma((NL,)), dma((NL,)),
            dma((NL,)), dma((NL,)),
            dma((NP,)), dma((NP,)),
            dma((NZ,)), dma((NZ,)),
        ],
        compiler_params=pltpu.CompilerParams(
            collective_id=0, has_side_effects=True, vmem_limit_bytes=32 * 1024 * 1024
        ),
        name="routed_backward",
    )(
        expert_ids.T, row_slots.T, combine.T, grad_out,
        jnp.swapaxes(down_weight, 1, 2), gate_pre, up_pre,
    )
    return d_gate, d_up, d_combine.T


def solution(mesh):
    return jax.shard_map(
        shards,
        mesh=mesh,
        in_specs=(
            P("node", "local"),
            P(),
            P(),
            P(),
            P("node", None, "local"),
            P("node", None, "local"),
            P("node", None, "local"),
        ),
        out_specs=(P("node", None, "local"), P("node", None, "local"), P("node", None)),
        check_vma=False,
    )
```

```python
import jax
import jax.numpy as jnp
from jax import lax
from jax.experimental import pallas as pl
from jax.experimental.pallas import tpu as pltpu
from jax.sharding import PartitionSpec as P

MESH = pl.DeviceIdType.MESH
NP = 8
NZ = 16
NN = NP * NZ
NL = 8
CAP = 128
HB = 128
DL = 448
DPAD = 512
F32 = jnp.float32
BF16 = jnp.bfloat16
EXACT = lax.Precision.HIGHEST


def dot(a, b):
    return jnp.dot(a, b, preferred_element_type=F32)


def one_hot(cond, dtype=BF16):
    return jnp.where(cond, 1.0, 0.0).astype(dtype)


def iota(shape, dim):
    return lax.broadcasted_iota(jnp.int32, shape, dim)


def quantize(t):
    top = jnp.maximum(jnp.max(jnp.abs(t), axis=0, keepdims=True), 1e-30)
    q = jnp.round(t * (32767.0 / top)).astype(jnp.int32).astype(jnp.int16)
    return q, top * (1.0 / 32767.0)


def turn(i):
    half = lax.div(i + 1, 2)
    return 4 + half * (1 - 2 * lax.rem(i, 2))


def kernel(
    ids_hbm, slots_hbm, comb_hbm, g_hbm, w_hbm, gate_hbm, up_hbm,
    dg_ref, du_ref, dc_ref,
    ids_ref, slots_ref, comb_ref, g_ref, gate_ref, up_ref,
    s1, r1, s2, r2, wv, xs, gm, gsel, a_gate, a_up, qs, qr, cs, cr, acc,
    ys, yr, ps, pr, zs, zr, hs, hr, hcs, hcr, vv,
    in_sem, s1_sem, r1_sem, s2_sem, r2_sem, qs_sem, qr_sem, cs_sem, cr_sem,
    ys_sem, yr_sem, ps_sem, pr_sem, zs_sem, zr_sem, hs_sem, hr_sem, hcs_sem, hcr_sem,
):
    node = lax.axis_index("node")
    loc = lax.axis_index("local")
    zi = lax.div(node, NP)
    pi = lax.rem(node, NP)

    loads = [
        pltpu.make_async_copy(src, dst, in_sem.at[n])
        for n, (src, dst) in enumerate(
            (
                (ids_hbm, ids_ref), (g_hbm, g_ref), (slots_hbm, slots_ref), (comb_hbm, comb_ref),
                (gate_hbm, gate_ref), (up_hbm, up_ref), (w_hbm, wv),
            )
        )
    ]
    for load in loads:
        load.start()

    def p_peer(d):
        return lax.rem(pi + d, NP)

    def z_peer(d):
        return lax.rem(zi + d, NZ)

    def l_peer(d):
        return lax.rem(loc + d, NL)

    barrier = pltpu.get_barrier_semaphore()

    def greet_p(d, c):
        pl.semaphore_signal(barrier, inc=1, device_id=(zi * NP + p_peer(d), loc), device_id_type=MESH)
        pl.semaphore_signal(barrier, inc=1, device_id=(node, l_peer(d)), device_id_type=MESH)
        return c

    def greet_z(d, c):
        pl.semaphore_signal(barrier, inc=1, device_id=(z_peer(d) * NP + pi, loc), device_id_type=MESH)
        return c

    lax.fori_loop(1, NP, greet_p, 0)
    lax.fori_loop(1, NZ, greet_z, 0)

    loads[0].wait()
    loads[1].wait()
    base = pl.multiple_of(lax.div(node, 4) * 128, 128)
    ids_c = ids_ref[:, pl.ds(base, 128)]
    sub = lax.rem(node, 4)
    ids_my = ids_c[:, 0:32]
    for j in range(1, 4):
        ids_my = jnp.where(sub == j, ids_c[:, 32 * j : 32 * j + 32], ids_my)
    dest = ids_my >> 1
    i = iota((NN, 32), 0)
    dest_of = (i & (NZ - 1)) * NP + (i >> 4)
    hit = jnp.zeros((NN, 32), F32)
    for k in range(8):
        hit = jnp.where(dest_of == dest[k : k + 1, :], 1.0, hit)
    x = dot(hit.astype(BF16), g_ref[...]).astype(BF16)
    s1[:, :, 0:DL] = x.reshape(NP, NZ, DL)
    s1[:, :, DL:DPAD] = jnp.zeros((NP, NZ, DPAD - DL), BF16)

    loads[4].wait()
    loads[5].wait()
    for e in range(2):
        g = gate_ref[e].astype(F32)
        u = up_ref[e].astype(F32)
        sg = 1.0 / (1.0 + jnp.exp(-g))
        gs = g * sg
        a_up[e] = gs
        a_gate[e] = u * sg * (1.0 + g * (1.0 - sg))
        q, scale = quantize(gs * u)
        hs[e] = q
        hcs[e : e + 1, :] = scale
    hr[pl.ds(loc, 1)] = hs[...].reshape(1, 2, CAP, HB)
    hcr[pl.ds(loc, 1)] = hcs[...].reshape(1, 2, HB)
    pl.semaphore_wait(barrier, 2 * (NP - 1) + NZ - 1)

    def s1_copy(d, src, dst):
        return pltpu.make_async_remote_copy(
            src_ref=s1.at[src], dst_ref=r1.at[dst],
            send_sem=s1_sem.at[d], recv_sem=r1_sem.at[d],
            device_id=(zi * NP + p_peer(d), loc), device_id_type=MESH,
        )

    def s1_start(d, c):
        s1_copy(d, p_peer(d), pi).start()
        return c

    lax.fori_loop(1, NP, s1_start, 0)
    r1[pl.ds(pi, 1)] = s1[pl.ds(pi, 1)]

    def h_copy(d, dst):
        return pltpu.make_async_remote_copy(
            src_ref=hs, dst_ref=hr.at[dst],
            send_sem=hs_sem.at[d], recv_sem=hr_sem.at[d],
            device_id=(node, l_peer(d)), device_id_type=MESH,
        )

    def hc_copy(d, dst):
        return pltpu.make_async_remote_copy(
            src_ref=hcs, dst_ref=hcr.at[dst],
            send_sem=hcs_sem.at[d], recv_sem=hcr_sem.at[d],
            device_id=(node, l_peer(d)), device_id_type=MESH,
        )

    def h_start(i, c):
        d = turn(i)
        hc_copy(d, loc).start()
        h_copy(d, loc).start()
        return c

    lax.fori_loop(0, NL - 1, h_start, 0)

    ri = iota((2 * NN, NN), 0)
    ci = iota((2 * NN, NN), 1)
    want = (ri & (NP - 1)) * NZ + (ri >> 4)
    half = (ri >> 3) & 1
    perm0 = one_hot((ci == want) & (half == 0))
    perm1 = one_hot((ci == want) & (half == 1))

    def s1_wait(d, c):
        s1_copy(d, p_peer(d), lax.rem(pi + NP - d, NP)).wait_recv()
        return c

    lax.fori_loop(1, NP, s1_wait, 0)
    r1f = r1[...].reshape(NN, DPAD)
    s2v = dot(perm0, r1f[:, 0:256]) + dot(perm1, r1f[:, 256:512])
    s2[...] = s2v.astype(BF16).reshape(NZ, 16, 256)

    def s2_copy(d, src, dst):
        return pltpu.make_async_remote_copy(
            src_ref=s2.at[src], dst_ref=r2.at[dst],
            send_sem=s2_sem.at[d], recv_sem=r2_sem.at[d],
            device_id=(z_peer(d) * NP + pi, loc), device_id_type=MESH,
        )

    def s2_start(d, c):
        s2_copy(d, z_peer(d), zi).start()
        return c

    lax.fori_loop(1, NZ, s2_start, 0)
    r2[pl.ds(zi, 1)] = s2[pl.ds(zi, 1)]

    loads[2].wait()
    loads[3].wait()
    ids = ids_ref[...]
    slots = slots_ref[...].astype(F32)
    comb = comb_ref[...]
    spread = (iota((128, NN), 0) >> 5) == (iota((128, NN), 1) & 3)
    spread_b = one_hot(spread)
    spread_f = one_hot(spread, F32)
    rows_here = (iota((256, NN), 0) >> 3) == (iota((256, NN), 1) >> 2)

    def stack(v):
        return jnp.concatenate([v[:, c * 128 : (c + 1) * 128] for c in range(32)], axis=0)

    nn = iota((NN, 256), 0)
    cc = iota((NN, 256), 1)
    place = (nn >> 3) * 16 + (nn & 7)
    ex0 = one_hot(cc == place)
    ex1 = one_hot(cc == place + 8)
    si = iota((CAP, NN), 0).astype(F32)
    for e in range(2):
        mine = ids == 2 * node + e
        slot_y = dot(stack(jnp.where(mine, slots, 0.0)).astype(BF16), spread_b)
        slot_n = jnp.sum(jnp.where(rows_here, slot_y, 0.0), axis=0, keepdims=True)
        comb_y = jnp.dot(
            stack(jnp.where(mine, comb, 0.0)), spread_f, precision=EXACT, preferred_element_type=F32
        )
        comb_n = jnp.sum(jnp.where(rows_here, comb_y, 0.0), axis=0, keepdims=True)
        sel = si == slot_n
        sel_f = jnp.where(sel, 1.0, 0.0)
        gm[e] = sel_f
        weight = jnp.sum(jnp.where(sel, comb_n, 0.0), axis=1, keepdims=True)
        sel_b = sel_f.astype(BF16)
        gsel[e, 0] = dot(sel_b, ex0).astype(BF16)
        gsel[e, 1] = dot(sel_b, ex1).astype(BF16)
        a_up[e] = weight * a_up[e]
        a_gate[e] = weight * a_gate[e]

    loads[6].wait()

    def h_wait(i, c):
        d = turn(i)
        l = lax.rem(loc + NL - d, NL)
        hc_copy(d, l).wait_recv()
        h_copy(d, l).wait_recv()
        return c

    lax.fori_loop(0, NL - 1, h_wait, 0)

    vv[...] = jnp.zeros((2, CAP, DL), F32)

    def back_project(j, c):
        cols = pl.ds(pl.multiple_of(j * 2 * HB, 2 * HB), 2 * HB)
        for e in range(2):
            h = jnp.concatenate(
                [
                    hr[2 * j + b, e].astype(jnp.int32).astype(F32) * hcr[2 * j + b, e : e + 1, :]
                    for b in range(2)
                ],
                axis=1,
            )
            top = h.astype(BF16)
            rest = (h - top.astype(F32)).astype(BF16)
            r = lax.dot_general(
                jnp.concatenate([top, rest], axis=0), wv[e, :, cols],
                (((1,), (1,)), ((), ())), preferred_element_type=F32,
            )
            vv[e] += r[:CAP] + r[CAP:]
        return c

    lax.fori_loop(0, NL // 2, back_project, 0)

    def s2_wait(d, c):
        s2_copy(d, z_peer(d), lax.rem(zi + NZ - d, NZ)).wait_recv()
        return c

    lax.fori_loop(1, NZ, s2_wait, 0)
    r2f = r2[...].reshape(256, 256)
    for e in range(2):
        xs[e, :, 0:256] = dot(gsel[e, 0], r2f).astype(BF16)
        xs[e, :, 256:512] = dot(gsel[e, 1], r2f).astype(BF16)
    for e in range(2):
        part = jnp.sum(xs[e, :, 0:DL].astype(F32) * vv[e], axis=1, keepdims=True)
        ys[e : e + 1, :] = jnp.sum(gm[e] * part, axis=0, keepdims=True)

    def y_copy(d, dst):
        return pltpu.make_async_remote_copy(
            src_ref=ys, dst_ref=yr.at[dst],
            send_sem=ys_sem.at[d], recv_sem=yr_sem.at[d],
            device_id=(node, l_peer(d)), device_id_type=MESH,
        )

    def y_start(i, c):
        y_copy(turn(i), loc).start()
        return c

    lax.fori_loop(0, NL - 1, y_start, 0)
    yr[pl.ds(loc, 1)] = ys[...].reshape(1, 2, NN)

    def q_copy(d, src, dst):
        return pltpu.make_async_remote_copy(
            src_ref=qs.at[src], dst_ref=qr.at[dst],
            send_sem=qs_sem.at[d], recv_sem=qr_sem.at[d],
            device_id=(node, l_peer(d)), device_id_type=MESH,
        )

    def c_copy(d, src, dst):
        return pltpu.make_async_remote_copy(
            src_ref=cs.at[src], dst_ref=cr.at[dst],
            send_sem=cs_sem.at[d], recv_sem=cr_sem.at[d],
            device_id=(node, l_peer(d)), device_id_type=MESH,
        )

    def project(e, l):
        cols = pl.ds(pl.multiple_of(l * HB, HB), HB)
        return dot(xs[e, :, 0:DL], wv[e, :, cols])

    def send_block(i, c):
        d = turn(i)
        l = l_peer(d)
        for e in range(2):
            t = project(e, l)
            q, scale = quantize(t)
            qs[l, e] = q
            cs[l, e : e + 1, :] = scale
        c_copy(d, l, loc).start()
        q_copy(d, l, loc).start()
        return c

    lax.fori_loop(0, NL - 1, send_block, 0)
    for e in range(2):
        acc[e] = project(e, loc)

    def y_wait(d, c):
        y_copy(d, lax.rem(loc + NL - d, NL)).wait_recv()
        return c

    lax.fori_loop(1, NL, y_wait, 0)
    ps[...] = jnp.sum(yr[...], axis=0)

    def p_copy(d, dst):
        return pltpu.make_async_remote_copy(
            src_ref=ps, dst_ref=pr.at[dst],
            send_sem=ps_sem.at[d], recv_sem=pr_sem.at[d],
            device_id=(zi * NP + p_peer(d), loc), device_id_type=MESH,
        )

    def p_start(d, c):
        p_copy(d, pi).start()
        return c

    lax.fori_loop(1, NP, p_start, 0)
    pr[pl.ds(pi, 1)] = ps[...].reshape(1, 2, NN)

    def p_wait(d, c):
        p_copy(d, lax.rem(pi + NP - d, NP)).wait_recv()
        return c

    lax.fori_loop(1, NP, p_wait, 0)
    to_here = (iota((2, NN), 1) & (NP - 1)) == pi
    packed = jnp.zeros((2, NN), F32)
    for q in range(NP):
        v = jnp.where(to_here, pr[q], 0.0)
        if q:
            v = jnp.concatenate([v[:, NN - q :], v[:, : NN - q]], axis=1)
        packed = packed + v
    zs[...] = packed

    def z_copy(d, dst):
        return pltpu.make_async_remote_copy(
            src_ref=zs, dst_ref=zr.at[dst],
            send_sem=zs_sem.at[d], recv_sem=zr_sem.at[d],
            device_id=(z_peer(d) * NP + pi, loc), device_id_type=MESH,
        )

    def z_start(d, c):
        z_copy(d, zi).start()
        return c

    lax.fori_loop(1, NZ, z_start, 0)
    zr[pl.ds(zi, 1)] = packed.reshape(1, 2, NN)

    def take_block(i, c):
        d = turn(i)
        l = lax.rem(loc + NL - d, NL)
        c_copy(d, l_peer(d), l).wait_recv()
        q_copy(d, l_peer(d), l).wait_recv()
        for e in range(2):
            acc[e] += qr[l, e].astype(jnp.int32).astype(F32) * cr[l, e : e + 1, :]
        return c

    lax.fori_loop(0, NL - 1, take_block, 0)

    for e in range(2):
        t = acc[e]
        dg_ref[e] = (t * a_gate[e]).astype(BF16)
        du_ref[e] = (t * a_up[e]).astype(BF16)

    choice = jnp.concatenate([ids_my[k : k + 1, :] for k in range(8)], axis=1)
    lane = (node + ((choice >> 1) & (NP - 1))) & (NN - 1)
    lane_hit = iota((NN, 256), 0) == lane
    plane_hit = iota((NZ, 256), 0) == (choice >> 4)
    member = choice & 1

    def z_wait(d, c):
        z_copy(d, lax.rem(zi + NZ - d, NZ)).wait_recv()
        return c

    lax.fori_loop(1, NZ, z_wait, 0)
    found = jnp.zeros((NN, 256), F32)
    for m in range(2):
        pick = jnp.where(plane_hit & (member == m), 1.0, 0.0)
        found = found + lax.dot_general(
            zr[:, m, :], pick, (((0,), (0,)), ((), ())), precision=EXACT, preferred_element_type=F32
        )
    flat = jnp.sum(jnp.where(lane_hit, found, 0.0), axis=0, keepdims=True)
    for k in range(8):
        dc_ref[k : k + 1, :] = flat[:, 32 * k : 32 * k + 32]

    def drain8(d, c):
        s1_copy(d, p_peer(d), pi).wait_send()
        q_copy(d, l_peer(d), loc).wait_send()
        c_copy(d, l_peer(d), loc).wait_send()
        y_copy(d, loc).wait_send()
        h_copy(d, loc).wait_send()
        hc_copy(d, loc).wait_send()
        p_copy(d, pi).wait_send()
        return c

    def drain16(d, c):
        s2_copy(d, z_peer(d), zi).wait_send()
        z_copy(d, zi).wait_send()
        return c

    lax.fori_loop(1, NP, drain8, 0)
    lax.fori_loop(1, NZ, drain16, 0)


def shards(grad_out, expert_ids, row_slots, combine, down_weight, gate_pre, up_pre):
    vmem = pl.BlockSpec(memory_space=pltpu.VMEM)
    dma = pltpu.SemaphoreType.DMA
    d_gate, d_up, d_combine = pl.pallas_call(
        kernel,
        out_shape=(
            jax.ShapeDtypeStruct(gate_pre.shape, BF16),
            jax.ShapeDtypeStruct(gate_pre.shape, BF16),
            jax.ShapeDtypeStruct((8, 32), F32),
        ),
        in_specs=[pl.BlockSpec(memory_space=pltpu.HBM)] * 7,
        out_specs=(vmem, vmem, vmem),
        scratch_shapes=[
            pltpu.VMEM((8, 4096), jnp.int32),
            pltpu.VMEM((8, 4096), jnp.int32),
            pltpu.VMEM((8, 4096), F32),
            pltpu.VMEM((32, DL), BF16),
            pltpu.VMEM((2, CAP, HB), BF16),
            pltpu.VMEM((2, CAP, HB), BF16),
            pltpu.VMEM((NP, NZ, DPAD), BF16),
            pltpu.VMEM((NP, NZ, DPAD), BF16),
            pltpu.VMEM((NZ, 16, 256), BF16),
            pltpu.VMEM((NZ, 16, 256), BF16),
            pltpu.VMEM((2, DL, 1024), BF16),
            pltpu.VMEM((2, CAP, DPAD), BF16),
            pltpu.VMEM((2, CAP, NN), F32),
            pltpu.VMEM((2, 2, CAP, 256), BF16),
            pltpu.VMEM((2, CAP, HB), F32),
            pltpu.VMEM((2, CAP, HB), F32),
            pltpu.VMEM((NL, 2, CAP, HB), jnp.int16),
            pltpu.VMEM((NL, 2, CAP, HB), jnp.int16),
            pltpu.VMEM((NL, 2, HB), F32),
            pltpu.VMEM((NL, 2, HB), F32),
            pltpu.VMEM((2, CAP, HB), F32),
            pltpu.VMEM((2, NN), F32),
            pltpu.VMEM((NL, 2, NN), F32),
            pltpu.VMEM((2, NN), F32),
            pltpu.VMEM((NP, 2, NN), F32),
            pltpu.VMEM((2, NN), F32),
            pltpu.VMEM((NZ, 2, NN), F32),
            pltpu.VMEM((2, CAP, HB), jnp.int16),
            pltpu.VMEM((NL, 2, CAP, HB), jnp.int16),
            pltpu.VMEM((2, HB), F32),
            pltpu.VMEM((NL, 2, HB), F32),
            pltpu.VMEM((2, CAP, DL), F32),
            dma((7,)),
            dma((NP,)), dma((NP,)),
            dma((NZ,)), dma((NZ,)),
            dma((NL,)), dma((NL,)),
            dma((NL,)), dma((NL,)),
            dma((NL,)), dma((NL,)),
            dma((NP,)), dma((NP,)),
            dma((NZ,)), dma((NZ,)),
            dma((NL,)), dma((NL,)),
            dma((NL,)), dma((NL,)),
        ],
        compiler_params=pltpu.CompilerParams(
            collective_id=0, has_side_effects=True, vmem_limit_bytes=60 * 1024 * 1024
        ),
        name="routed_backward",
    )(
        expert_ids.T, row_slots.T, combine.T, grad_out,
        jnp.swapaxes(down_weight, 1, 2), gate_pre, up_pre,
    )
    return d_gate, d_up, d_combine.T


def solution(mesh):
    return jax.shard_map(
        shards,
        mesh=mesh,
        in_specs=(
            P("node", "local"),
            P(),
            P(),
            P(),
            P("node", None, "local"),
            P("node", None, "local"),
            P("node", None, "local"),
        ),
        out_specs=(P("node", None, "local"), P("node", None, "local"), P("node", None)),
        check_vma=False,
    )
```

```python
import jax
import jax.numpy as jnp
from jax import lax
from jax.experimental import pallas as pl
from jax.experimental.pallas import tpu as pltpu
from jax.sharding import PartitionSpec as P

MESH = pl.DeviceIdType.MESH
NP = 8
NZ = 16
NN = NP * NZ
NL = 8
CAP = 128
HB = 128
DL = 448
DPAD = 512
F32 = jnp.float32
BF16 = jnp.bfloat16
EXACT = lax.Precision.HIGHEST


def dot(a, b):
    return jnp.dot(a, b, preferred_element_type=F32)


def one_hot(cond, dtype=BF16):
    return jnp.where(cond, 1.0, 0.0).astype(dtype)


def iota(shape, dim):
    return lax.broadcasted_iota(jnp.int32, shape, dim)


def quantize(t):
    top = jnp.maximum(jnp.max(jnp.abs(t), axis=0, keepdims=True), 1e-30)
    q = jnp.round(t * (32767.0 / top)).astype(jnp.int32).astype(jnp.int16)
    return q, top * (1.0 / 32767.0)


def turn(i):
    half = lax.div(i + 1, 2)
    return 4 + half * (1 - 2 * lax.rem(i, 2))


def z_turn(i):
    half = lax.div(i + 1, 2)
    return 8 + half * (1 - 2 * lax.rem(i, 2))


def kernel(
    ids_hbm, slots_hbm, comb_hbm, g_hbm, w_hbm, gate_hbm, up_hbm,
    dg_ref, du_ref, dc_ref,
    near_ref, ids_ref, slots_ref, comb_ref, g_ref, gate_ref, up_ref,
    s1, r1, s2, r2, wv, xs, gm, gsel, a_gate, a_up, qs, qr, cs, cr, acc,
    ys, yr, zs, zr, hs, hr, hcs, hcr, vv,
    in_sem, s1_sem, r1_sem, s2_sem, r2_sem, qs_sem, qr_sem, cs_sem, cr_sem,
    higher, ys_sem, yr_sem, zs_sem, zr_sem, hs_sem, hr_sem, hcs_sem, hcr_sem,
):
    node = lax.axis_index("node")
    loc = lax.axis_index("local")
    zi = lax.div(node, NP)
    pi = lax.rem(node, NP)

    base = pl.multiple_of(lax.div(node, 4) * 128, 128)
    loads = [
        pltpu.make_async_copy(src, dst, in_sem.at[n])
        for n, (src, dst) in enumerate(
            (
                (ids_hbm.at[:, pl.ds(base, 128)], near_ref), (g_hbm, g_ref),
                (slots_hbm, slots_ref), (comb_hbm, comb_ref),
                (gate_hbm, gate_ref), (up_hbm, up_ref), (w_hbm, wv), (ids_hbm, ids_ref),
            )
        )
    ]
    for n in (0, 1, 4, 5, 7, 2, 3, 6):
        loads[n].start()

    def p_peer(d):
        return lax.rem(pi + d, NP)

    def z_peer(d):
        return lax.rem(zi + d, NZ)

    def l_peer(d):
        return lax.rem(loc + d, NL)

    late = jnp.where(jnp.logical_and(pi == 0, loc == 0), 1, 0)
    rank = lax.rem(zi + late * (NZ - 1), NZ)

    def plane(r):
        return lax.rem(r + late, NZ)

    def rank_of(z):
        return lax.rem(z + late * (NZ - 1), NZ)

    barrier = pltpu.get_barrier_semaphore()

    def greet_p(d, c):
        pl.semaphore_signal(barrier, inc=1, device_id=(zi * NP + p_peer(d), loc), device_id_type=MESH)
        pl.semaphore_signal(barrier, inc=1, device_id=(node, l_peer(d)), device_id_type=MESH)
        return c

    def greet_z(k, c):
        pl.semaphore_signal(barrier, inc=1, device_id=(plane(k) * NP + pi, loc), device_id_type=MESH)
        return c

    def answer_z(k, c):
        pl.semaphore_signal(higher, inc=1, device_id=(plane(k) * NP + pi, loc), device_id_type=MESH)
        return c

    lax.fori_loop(1, NP, greet_p, 0)
    lax.fori_loop(rank + 1, NZ, greet_z, 0)
    pl.semaphore_wait(barrier, 2 * (NP - 1) + rank)
    lax.fori_loop(0, rank, answer_z, 0)

    loads[0].wait()
    loads[1].wait()
    ids_c = near_ref[...]
    sub = lax.rem(node, 4)
    ids_my = ids_c[:, 0:32]
    for j in range(1, 4):
        ids_my = jnp.where(sub == j, ids_c[:, 32 * j : 32 * j + 32], ids_my)
    dest = ids_my >> 1
    i = iota((NN, 32), 0)
    dest_of = (i & (NZ - 1)) * NP + (i >> 4)
    hit = jnp.zeros((NN, 32), F32)
    for k in range(8):
        hit = jnp.where(dest_of == dest[k : k + 1, :], 1.0, hit)
    x = dot(hit.astype(BF16), g_ref[...]).astype(BF16)
    s1[:, :, 0:DL] = x.reshape(NP, NZ, DL)
    s1[:, :, DL:DPAD] = jnp.zeros((NP, NZ, DPAD - DL), BF16)


    def s1_copy(d, src, dst):
        return pltpu.make_async_remote_copy(
            src_ref=s1.at[src], dst_ref=r1.at[dst],
            send_sem=s1_sem.at[d], recv_sem=r1_sem.at[d],
            device_id=(zi * NP + p_peer(d), loc), device_id_type=MESH,
        )

    def s1_start(d, c):
        s1_copy(d, p_peer(d), pi).start()
        return c

    lax.fori_loop(1, NP, s1_start, 0)
    r1[pl.ds(pi, 1)] = s1[pl.ds(pi, 1)]

    loads[4].wait()
    loads[5].wait()
    for e in range(2):
        g = gate_ref[e].astype(F32)
        u = up_ref[e].astype(F32)
        sg = 1.0 / (1.0 + jnp.exp(-g))
        gs = g * sg
        a_up[e] = gs
        a_gate[e] = u * sg * (1.0 + g * (1.0 - sg))
        q, scale = quantize(gs * u)
        hs[e] = q
        hcs[e : e + 1, :] = scale
    hr[pl.ds(loc, 1)] = hs[...].reshape(1, 2, CAP, HB)
    hcr[pl.ds(loc, 1)] = hcs[...].reshape(1, 2, HB)

    def h_copy(d, dst):
        return pltpu.make_async_remote_copy(
            src_ref=hs, dst_ref=hr.at[dst],
            send_sem=hs_sem.at[d], recv_sem=hr_sem.at[d],
            device_id=(node, l_peer(d)), device_id_type=MESH,
        )

    def hc_copy(d, dst):
        return pltpu.make_async_remote_copy(
            src_ref=hcs, dst_ref=hcr.at[dst],
            send_sem=hcs_sem.at[d], recv_sem=hcr_sem.at[d],
            device_id=(node, l_peer(d)), device_id_type=MESH,
        )

    def h_start(i, c):
        d = turn(i)
        hc_copy(d, loc).start()
        h_copy(d, loc).start()
        return c

    lax.fori_loop(0, NL - 1, h_start, 0)

    ri = iota((2 * NN, NN), 0)
    ci = iota((2 * NN, NN), 1)
    want = (ri & (NP - 1)) * NZ + (ri >> 4)
    half = (ri >> 3) & 1
    perm0 = one_hot((ci == want) & (half == 0))
    perm1 = one_hot((ci == want) & (half == 1))

    def s1_wait(d, c):
        s1_copy(d, p_peer(d), lax.rem(pi + NP - d, NP)).wait_recv()
        return c

    lax.fori_loop(1, NP, s1_wait, 0)
    r1f = r1[...].reshape(NN, DPAD)
    s2v = dot(perm0, r1f[:, 0:256]) + dot(perm1, r1f[:, 256:512])
    s2[...] = s2v.astype(BF16).reshape(NZ, 16, 256)

    def s2_copy(d, src, dst):
        return pltpu.make_async_remote_copy(
            src_ref=s2.at[src], dst_ref=r2.at[dst],
            send_sem=s2_sem.at[d], recv_sem=r2_sem.at[d],
            device_id=(z_peer(d) * NP + pi, loc), device_id_type=MESH,
        )

    def s2_start(d):
        s2_copy(d, z_peer(d), zi).start()

    def s2_lower(i, c):
        d = z_turn(i)
        pl.when(rank_of(z_peer(d)) < rank)(lambda: s2_start(d))
        return c

    def s2_higher(i, c):
        d = z_turn(i)
        pl.when(rank_of(z_peer(d)) > rank)(lambda: s2_start(d))
        return c

    lax.fori_loop(0, NZ - 1, s2_lower, 0)
    pl.when(rank < NZ - 1)(lambda: pl.semaphore_wait(higher, NZ - 1 - rank))
    lax.fori_loop(0, NZ - 1, s2_higher, 0)
    r2[pl.ds(zi, 1)] = s2[pl.ds(zi, 1)]

    loads[7].wait()
    loads[2].wait()
    loads[3].wait()
    ids = ids_ref[...]
    slots = slots_ref[...].astype(F32)
    comb = comb_ref[...]
    spread = (iota((128, NN), 0) >> 5) == (iota((128, NN), 1) & 3)
    spread_b = one_hot(spread)
    spread_f = one_hot(spread, F32)
    rows_here = (iota((256, NN), 0) >> 3) == (iota((256, NN), 1) >> 2)

    def stack(v):
        return jnp.concatenate([v[:, c * 128 : (c + 1) * 128] for c in range(32)], axis=0)

    nn = iota((NN, 256), 0)
    cc = iota((NN, 256), 1)
    place = (nn >> 3) * 16 + (nn & 7)
    ex0 = one_hot(cc == place)
    ex1 = one_hot(cc == place + 8)
    si = iota((CAP, NN), 0).astype(F32)
    for e in range(2):
        mine = ids == 2 * node + e
        slot_y = dot(stack(jnp.where(mine, slots, 0.0)).astype(BF16), spread_b)
        slot_n = jnp.sum(jnp.where(rows_here, slot_y, 0.0), axis=0, keepdims=True)
        comb_y = jnp.dot(
            stack(jnp.where(mine, comb, 0.0)), spread_f, precision=EXACT, preferred_element_type=F32
        )
        comb_n = jnp.sum(jnp.where(rows_here, comb_y, 0.0), axis=0, keepdims=True)
        sel = si == slot_n
        sel_f = jnp.where(sel, 1.0, 0.0)
        gm[e] = sel_f
        weight = jnp.sum(jnp.where(sel, comb_n, 0.0), axis=1, keepdims=True)
        sel_b = sel_f.astype(BF16)
        gsel[e, 0] = dot(sel_b, ex0).astype(BF16)
        gsel[e, 1] = dot(sel_b, ex1).astype(BF16)
        a_up[e] = weight * a_up[e]
        a_gate[e] = weight * a_gate[e]

    loads[6].wait()

    def back_project(l, first):
        cols = pl.ds(pl.multiple_of(l * HB, HB), HB)
        for e in range(2):
            h = hr[l, e].astype(jnp.int32).astype(F32) * hcr[l, e : e + 1, :]
            top = h.astype(BF16)
            rest = (h - top.astype(F32)).astype(BF16)
            r = lax.dot_general(
                jnp.concatenate([top, rest], axis=0), wv[e, :, cols],
                (((1,), (1,)), ((), ())), preferred_element_type=F32,
            )
            r = r[:CAP] + r[CAP:]
            if first:
                vv[e] = r
            else:
                vv[e] += r

    def h_take(i, c):
        d = turn(i)
        l = lax.rem(loc + NL - d, NL)
        hc_copy(d, l).wait_recv()
        h_copy(d, l).wait_recv()
        back_project(l, False)
        return c

    back_project(loc, True)
    lax.fori_loop(0, NL - 1, h_take, 0)

    def s2_wait(d, c):
        s2_copy(d, z_peer(d), lax.rem(zi + NZ - d, NZ)).wait_recv()
        return c

    lax.fori_loop(1, NZ, s2_wait, 0)
    r2f = r2[...].reshape(256, 256)
    for e in range(2):
        xs[e, :, 0:256] = dot(gsel[e, 0], r2f).astype(BF16)
        xs[e, :, 256:512] = dot(gsel[e, 1], r2f).astype(BF16)
    for e in range(2):
        part = jnp.sum(xs[e, :, 0:DL].astype(F32) * vv[e], axis=1, keepdims=True)
        ys[e : e + 1, :] = jnp.sum(gm[e] * part, axis=0, keepdims=True)

    def y_copy(i):
        dp, dl = lax.div(i, NL), lax.rem(i, NL)
        return pltpu.make_async_remote_copy(
            src_ref=ys, dst_ref=yr.at[i],
            send_sem=ys_sem.at[i], recv_sem=yr_sem.at[i],
            device_id=(zi * NP + p_peer(dp), l_peer(dl)), device_id_type=MESH,
        )

    def y_start(i, c):
        y_copy(i).start()
        return c

    lax.fori_loop(1, NP * NL, y_start, 0)
    yr[0] = ys[...]

    def q_copy(d, src, dst):
        return pltpu.make_async_remote_copy(
            src_ref=qs.at[src], dst_ref=qr.at[dst],
            send_sem=qs_sem.at[d], recv_sem=qr_sem.at[d],
            device_id=(node, l_peer(d)), device_id_type=MESH,
        )

    def c_copy(d, src, dst):
        return pltpu.make_async_remote_copy(
            src_ref=cs.at[src], dst_ref=cr.at[dst],
            send_sem=cs_sem.at[d], recv_sem=cr_sem.at[d],
            device_id=(node, l_peer(d)), device_id_type=MESH,
        )

    def project(e, l):
        cols = pl.ds(pl.multiple_of(l * HB, HB), HB)
        return dot(xs[e, :, 0:DL], wv[e, :, cols])

    def send_block(i, c):
        d = turn(i)
        l = l_peer(d)
        for e in range(2):
            t = project(e, l)
            q, scale = quantize(t)
            qs[l, e] = q
            cs[l, e : e + 1, :] = scale
        c_copy(d, l, loc).start()
        q_copy(d, l, loc).start()
        return c

    lax.fori_loop(0, NL - 1, send_block, 0)
    for e in range(2):
        acc[e] = project(e, loc)

    def y_wait(i, c):
        y_copy(i).wait_recv()
        return c

    lax.fori_loop(1, NP * NL, y_wait, 0)
    to_here = (iota((2, NN), 1) & (NP - 1)) == pi
    packed = jnp.zeros((2, NN), F32)
    for q in range(NP):
        v = jnp.where(to_here, jnp.sum(yr[q * NL : (q + 1) * NL], axis=0), 0.0)
        if q:
            v = jnp.concatenate([v[:, NN - q :], v[:, : NN - q]], axis=1)
        packed = packed + v
    zs[...] = packed

    def z_copy(d, dst):
        return pltpu.make_async_remote_copy(
            src_ref=zs, dst_ref=zr.at[dst],
            send_sem=zs_sem.at[d], recv_sem=zr_sem.at[d],
            device_id=(z_peer(d) * NP + pi, loc), device_id_type=MESH,
        )

    def z_start(i, c):
        z_copy(z_turn(i), zi).start()
        return c

    lax.fori_loop(0, NZ - 1, z_start, 0)
    zr[pl.ds(zi, 1)] = packed.reshape(1, 2, NN)

    def take_block(i, c):
        d = turn(i)
        l = lax.rem(loc + NL - d, NL)
        c_copy(d, l_peer(d), l).wait_recv()
        q_copy(d, l_peer(d), l).wait_recv()
        for e in range(2):
            acc[e] += qr[l, e].astype(jnp.int32).astype(F32) * cr[l, e : e + 1, :]
        return c

    lax.fori_loop(0, NL - 1, take_block, 0)

    for e in range(2):
        t = acc[e]
        dg_ref[e] = (t * a_gate[e]).astype(BF16)
        du_ref[e] = (t * a_up[e]).astype(BF16)

    choice = jnp.concatenate([ids_my[k : k + 1, :] for k in range(8)], axis=1)
    lane = (node + ((pi - (choice >> 1)) & (NP - 1))) & (NN - 1)
    lane_hit = iota((NN, 256), 0) == lane
    plane_hit = iota((NZ, 256), 0) == (choice >> 4)
    member = choice & 1

    def z_wait(d, c):
        z_copy(d, lax.rem(zi + NZ - d, NZ)).wait_recv()
        return c

    lax.fori_loop(1, NZ, z_wait, 0)
    found = jnp.zeros((NN, 256), F32)
    for m in range(2):
        pick = jnp.where(plane_hit & (member == m), 1.0, 0.0)
        found = found + lax.dot_general(
            zr[:, m, :], pick, (((0,), (0,)), ((), ())), precision=EXACT, preferred_element_type=F32
        )
    flat = jnp.sum(jnp.where(lane_hit, found, 0.0), axis=0, keepdims=True)
    for k in range(8):
        dc_ref[k : k + 1, :] = flat[:, 32 * k : 32 * k + 32]

    def drain8(d, c):
        s1_copy(d, p_peer(d), pi).wait_send()
        q_copy(d, l_peer(d), loc).wait_send()
        c_copy(d, l_peer(d), loc).wait_send()
        h_copy(d, loc).wait_send()
        hc_copy(d, loc).wait_send()
        return c

    def drain16(d, c):
        s2_copy(d, z_peer(d), zi).wait_send()
        z_copy(d, zi).wait_send()
        return c

    def drain64(i, c):
        y_copy(i).wait_send()
        return c

    lax.fori_loop(1, NP, drain8, 0)
    lax.fori_loop(1, NP * NL, drain64, 0)
    lax.fori_loop(1, NZ, drain16, 0)


def shards(grad_out, expert_ids, row_slots, combine, down_weight, gate_pre, up_pre):
    vmem = pl.BlockSpec(memory_space=pltpu.VMEM)
    dma = pltpu.SemaphoreType.DMA
    d_gate, d_up, d_combine = pl.pallas_call(
        kernel,
        out_shape=(
            jax.ShapeDtypeStruct(gate_pre.shape, BF16),
            jax.ShapeDtypeStruct(gate_pre.shape, BF16),
            jax.ShapeDtypeStruct((8, 32), F32),
        ),
        in_specs=[pl.BlockSpec(memory_space=pltpu.HBM)] * 7,
        out_specs=(vmem, vmem, vmem),
        scratch_shapes=[
            pltpu.VMEM((8, 128), jnp.int32),
            pltpu.VMEM((8, 4096), jnp.int32),
            pltpu.VMEM((8, 4096), jnp.int32),
            pltpu.VMEM((8, 4096), F32),
            pltpu.VMEM((32, DL), BF16),
            pltpu.VMEM((2, CAP, HB), BF16),
            pltpu.VMEM((2, CAP, HB), BF16),
            pltpu.VMEM((NP, NZ, DPAD), BF16),
            pltpu.VMEM((NP, NZ, DPAD), BF16),
            pltpu.VMEM((NZ, 16, 256), BF16),
            pltpu.VMEM((NZ, 16, 256), BF16),
            pltpu.VMEM((2, DL, 1024), BF16),
            pltpu.VMEM((2, CAP, DPAD), BF16),
            pltpu.VMEM((2, CAP, NN), F32),
            pltpu.VMEM((2, 2, CAP, 256), BF16),
            pltpu.VMEM((2, CAP, HB), F32),
            pltpu.VMEM((2, CAP, HB), F32),
            pltpu.VMEM((NL, 2, CAP, HB), jnp.int16),
            pltpu.VMEM((NL, 2, CAP, HB), jnp.int16),
            pltpu.VMEM((NL, 2, HB), F32),
            pltpu.VMEM((NL, 2, HB), F32),
            pltpu.VMEM((2, CAP, HB), F32),
            pltpu.VMEM((2, NN), F32),
            pltpu.VMEM((NP * NL, 2, NN), F32),
            pltpu.VMEM((2, NN), F32),
            pltpu.VMEM((NZ, 2, NN), F32),
            pltpu.VMEM((2, CAP, HB), jnp.int16),
            pltpu.VMEM((NL, 2, CAP, HB), jnp.int16),
            pltpu.VMEM((2, HB), F32),
            pltpu.VMEM((NL, 2, HB), F32),
            pltpu.VMEM((2, CAP, DL), F32),
            dma((8,)),
            dma((NP,)), dma((NP,)),
            dma((NZ,)), dma((NZ,)),
            dma((NL,)), dma((NL,)),
            dma((NL,)), dma((NL,)),
            pltpu.SemaphoreType.REGULAR,
            dma((NP * NL,)), dma((NP * NL,)),
            dma((NZ,)), dma((NZ,)),
            dma((NL,)), dma((NL,)),
            dma((NL,)), dma((NL,)),
        ],
        compiler_params=pltpu.CompilerParams(
            collective_id=0, has_side_effects=True, vmem_limit_bytes=60 * 1024 * 1024
        ),
        name="routed_backward",
    )(
        expert_ids.T, row_slots.T, combine.T, grad_out,
        jnp.swapaxes(down_weight, 1, 2), gate_pre, up_pre,
    )
    return d_gate, d_up, d_combine.T


def solution(mesh):
    return jax.shard_map(
        shards,
        mesh=mesh,
        in_specs=(
            P("node", "local"),
            P(),
            P(),
            P(),
            P("node", None, "local"),
            P("node", None, "local"),
            P("node", None, "local"),
        ),
        out_specs=(P("node", None, "local"), P("node", None, "local"), P("node", None)),
        check_vma=False,
    )
```
